512 devices in a mesh: side: 8 (over y_lo, x), ep: 8 (over y_hi, core), tp: 8 (over z).
Axes of the slice: x: 4, y: 8 (y_hi: 4, y_lo: 2; y = y_hi * 2 + y_lo), z: 8, core: 2. Of those that a mesh axis runs over, the one named last changes fastest.
Arguments:
- rows: bfloat16 [512, 6144], P(('ep', 'tp'), 'side'), may hold values from -6 to 6
- expert_ids: int32 [512, 2], P(('ep', 'tp')), may hold values from 0 to 7, all different within a row; in each aligned block of 8 rows (0 to 7, 8 to 15, ...) at most 4 rows name the same one
- combine: float32 [512, 2], P(('ep', 'tp')), may hold values from 0.2 to 1
- w_gate: bfloat16 [8, 6144, 8192], P('ep', 'side', 'tp'), may hold values from -0.078125 to 0.078125
- w_up: bfloat16 [8, 6144, 8192], P('ep', 'side', 'tp'), may hold values from -0.078125 to 0.078125
- w_down: bfloat16 [8, 8192, 6144], P('ep', 'tp', 'side'), may hold values from -0.0625 to 0.0625
Outputs:
- mixed: bfloat16 [512, 6144], P(('ep', 'tp'), 'side')
The draws below stay inside these ranges and needn't reach their ends.
Inputs may be any that keep to these rules, and one draw needn't show every extreme that they name: `expert_ids`: each row names 2 different experts; within the 8 rows of one device no expert is named by more than 4 rows, a bound that some block reaches.
All inputs are finite; a program needn't handle non-finite values.
Results may differ from the reference program's by a relative error of at most 0.034.
Values may be sent and summed in bfloat16 or wider, within the bound.
No kernel may reach another device: no remote copies, remote signals or barrier semaphores. Data moves between devices by JAX's collectives and lax.ppermute only.
A program may use at most 64 MiB of HBM per device.

```python
import math
import jax
import jax.numpy as jnp
import numpy as np
from jax import lax

D = 6144
FFW = 8192
TOP = 2
TOK_GRP = 8
EXPERTS = 8
CAP = 4
TOKENS = 512
N_SIDE = 8
N_EP = 8
N_TP = 8


def block_scale(stream_key, shape, cuts, low, high):
    loudness, own = 1.0, jax.random.fold_in(stream_key, 6)
    for dim, parts in cuts:
        heights = jnp.exp(jax.random.uniform(jax.random.fold_in(own, dim), (parts,), jnp.float32, low / len(cuts), high / len(cuts)))
        loudness = loudness * jnp.repeat(heights, shape[dim] // parts).reshape([-1 if axis == dim else 1 for axis in range(len(shape))])
    return loudness


def shared_out(own_key, own, number, rows, amount, top, most, skew):
    sequence = jax.random.permutation(own_key, amount)
    heavy_load, common = load_shares(amount, rows * top, most, skew, True), load_shares(amount, rows * top, most, skew, False)
    places = jnp.arange(amount)

    def named(tallies, offset_by):
        used = int((tallies > 0).sum())
        fixed = max(1, used // 4)
        shifted = fixed + (places - fixed + offset_by * (used - fixed)) % max(1, amount - fixed)
        return jnp.zeros((amount,), jnp.int32).at[sequence[jnp.where(places < fixed, places, shifted)]].set(jnp.asarray(tallies, jnp.int32))

    tallies = jnp.where(number % 4 == 0, named(heavy_load, number // 4), named(common, number - number // 4 - 1))
    mixed = jax.random.permutation(jax.random.fold_in(own, 3), amount)
    source_of, sink = mixed[0:amount // 2 * 2:2], mixed[1:amount // 2 * 2:2]
    room = jnp.minimum(tallies[source_of] - 1, most - tallies[sink]) // 2
    room = jnp.where((source_of == sequence[0]) | (sink == sequence[0]) | (tallies[sink] == 0), 0, jnp.maximum(room, 0))
    shifted = jax.random.randint(jax.random.fold_in(own, 4), (amount // 2,), 0, 1 << 20) % (room + 1)
    tallies = tallies.at[source_of].add(-shifted).at[sink].add(shifted)
    members = jnp.searchsorted(jnp.cumsum(tallies), jnp.arange(rows * top), side="right").astype(jnp.int32)
    table = members.reshape(top, rows).T
    table = table[jax.random.permutation(jax.random.fold_in(own, 1), rows)]
    offset_by = jax.random.randint(jax.random.fold_in(own, 2), (rows, 1), 0, top)
    return jnp.take_along_axis(table, (jnp.arange(top)[None, :] + offset_by) % top, axis=1)


def load_shares(amount, total, bound, skew, full):
    loads = [(1 << 20) // math.isqrt(grade ** skew) + 1 for grade in range(1, amount + 1)]
    largest = bound if full else min(bound, max(-(-total // amount), total * loads[0] // sum(loads)))
    least = 1 if total - largest >= amount - 1 else 0
    given, surplus = [largest] + [least] * (amount - 1), total - largest - least * (amount - 1)
    while surplus > 0:
        free = [i for i in range(1, amount) if given[i] < largest] or [i for i in range(1, amount) if given[i] < bound]
        whole, remaining = sum([loads[i] for i in free]), surplus
        for i in free:
            extra = min(bound - given[i], max(1, remaining * loads[i] // whole), surplus)
            given[i] = given[i] + extra
            surplus = surplus - extra
    return np.array(given)


def centred(own_key, extent, width, reach, shards=(), kind=jnp.bfloat16):
    drawn = jax.random.normal(own_key, extent, jnp.float32) * width
    if len(shards) > 0:
        drawn = block_scale(own_key, extent, shards, -0.22, 0.18) * drawn
    return jnp.clip(drawn, min=-reach, max=reach).astype(kind)


def setup_inputs(seed: int = 0) -> dict:
    splits = jax.random.split(jax.random.key(seed), 7)
    rows = centred(splits[0], (TOKENS, D), 1.0, 6.0, ((0, 64), (1, 8)))
    expert_ids_keys = jax.random.split(jax.random.fold_in(splits[1], 1), TOKENS // TOK_GRP)
    expert_ids_turns = jax.random.permutation(jax.random.fold_in(splits[1], 3), TOKENS // TOK_GRP)
    expert_ids = jax.vmap(lambda own, number: shared_out(jax.random.fold_in(splits[1], 2), own, number, TOK_GRP, EXPERTS, TOP, CAP, 2))(expert_ids_keys, expert_ids_turns).reshape((TOKENS, TOP))
    combine = jnp.clip(0.2 + 0.8 * jax.random.uniform(splits[2], (TOKENS, TOP), jnp.float32) ** block_scale(splits[2], (TOKENS, TOP), ((0, 64),), -0.2, 0.2), 0.2, 1.0)
    w_gate = centred(splits[3], (EXPERTS, D, FFW), D ** -0.5, 0.078125, ((0, 8), (1, 8), (2, 8)))
    w_up = centred(splits[4], (EXPERTS, D, FFW), D ** -0.5, 0.078125, ((0, 8), (1, 8), (2, 8)))
    w_down = centred(splits[5], (EXPERTS, FFW, D), FFW ** -0.5, 0.0625, ((0, 8), (1, 8), (2, 8)))
    return {"rows": rows, "expert_ids": expert_ids, "combine": combine, "w_gate": w_gate, "w_up": w_up, "w_down": w_down}


def reference(rows, expert_ids, combine, w_gate, w_up, w_down):
    tokens = rows.shape[0]
    slices = D // N_SIDE
    capacity = N_EP * N_TP * CAP
    chosen = expert_ids[:, :, None] == jnp.arange(EXPERTS, dtype=jnp.int32)[None, None, :]
    member = jnp.any(chosen, axis=1)
    ranking = jnp.cumsum(member.astype(jnp.int32), axis=0) - 1
    weighting = jnp.sum(combine[:, :, None] * chosen.astype(combine.dtype), axis=1)
    token_index = jnp.arange(tokens, dtype=jnp.int32)

    def expert_step(total, expert):
        inside = member[:, expert]
        place = jnp.where(inside, ranking[:, expert], capacity).astype(jnp.int32)
        table = jnp.zeros((capacity,), jnp.int32).at[place].set(token_index, mode="drop")
        picked = rows[table].reshape(capacity, N_SIDE, slices)
        picked = jnp.moveaxis(picked, 1, 0)
        gate_w = lax.dynamic_index_in_dim(w_gate, expert, 0, False).reshape(N_SIDE, slices, FFW)
        up_w = lax.dynamic_index_in_dim(w_up, expert, 0, False).reshape(N_SIDE, slices, FFW)

        def side_step(acc, items):
            block, gate_blk, up_blk = items
            gate_part = jnp.dot(block, gate_blk, preferred_element_type=jnp.float32).astype(jnp.bfloat16)
            up_part = jnp.dot(block, up_blk, preferred_element_type=jnp.float32).astype(jnp.bfloat16)
            gate_part, up_part = lax.optimization_barrier((gate_part, up_part))
            return (acc[0] + gate_part.astype(acc[0].dtype), acc[1] + up_part.astype(acc[1].dtype)), None

        start = jnp.zeros((capacity, FFW), jnp.float32)
        (gate, up), _ = lax.scan(side_step, (start, start), (picked, gate_w, up_w))
        hidden = (jax.nn.silu(gate) * up).astype(jnp.bfloat16)
        down_w = lax.dynamic_index_in_dim(w_down, expert, 0, False)
        expert_out = jnp.dot(hidden, down_w, preferred_element_type=jnp.float32).astype(jnp.bfloat16)
        back = expert_out[jnp.where(inside, ranking[:, expert], 0).astype(jnp.int32)]
        scale = jnp.where(inside, weighting[:, expert], 0.0)
        return total + scale[:, None] * back.astype(total.dtype), None

    total = jnp.zeros((tokens, D), jnp.float32)
    total, _ = lax.scan(expert_step, total, jnp.arange(EXPERTS, dtype=jnp.int32))
    return total.astype(jnp.bfloat16)
```

```python
import functools

import jax
import jax.numpy as jnp
from jax import lax
from jax.experimental import pallas as pl
from jax.experimental.pallas import tpu as pltpu
from jax.sharding import Mesh
from jax.sharding import PartitionSpec as P

BF, F32 = jnp.bfloat16, jnp.float32
VM = pl.BlockSpec(memory_space=pltpu.VMEM)
SM = pl.BlockSpec(memory_space=pltpu.SMEM)
LIMIT = pltpu.CompilerParams(vmem_limit_bytes=24 * 1024 * 1024)
CORES, HOSTS, TP, SIDE = 2, 4, 8, 8
TOK, CAP = 8, 4


def iota(shape, dim):
    return lax.broadcasted_iota(jnp.int32, shape, dim)


def route_kernel(core_ref, both_ref, out_ref, mix_ref):
    core = core_ref[0]
    both = both_ref[...]
    lane = iota((1, 128), 1)
    meta = jnp.where(iota((8, 128), 1) < 16, both[8:16, 0:128], both[24:32, 0:128])
    real = (iota((8, 128), 1) % 16 < TOK) & (iota((8, 128), 1) < 32)
    meta = jnp.where(real, meta, -1.0)
    row = iota((32, 128), 0)
    expert = (2 * (row // 8) + core).astype(F32)
    group, place = (row // CAP) % 2, (row % CAP).astype(F32)
    inside = ((meta[0:1] == expert) | (meta[1:2] == expert)) & (iota((32, 128), 1) // 16 == group)
    inside = inside.astype(F32)
    before = (iota((128, 128), 0) < iota((128, 128), 1)).astype(BF)
    rank = jnp.dot(inside.astype(BF), before, preferred_element_type=F32)
    pick = jnp.where(rank == place, inside, 0.0).astype(BF)
    slots = jnp.dot(pick[:, 0:32], both.astype(BF), preferred_element_type=F32)
    for h in range(HOSTS):
        mine = slots[8 * h : 8 * h + 8].astype(BF)
        for t in range(TP):
            out_ref[TP * h + t] = mine
    columns = jnp.transpose(meta)[0:32]
    spot = iota((32, 256), 1)
    expert = (2 * (spot // 64) + core).astype(F32)
    group, place = (spot // CAP) % 2, (spot % CAP).astype(F32)
    first, second = columns[:, 0:1] == expert, columns[:, 1:2] == expert
    inside = ((first | second) & (iota((32, 256), 0) // 16 == group)).astype(F32)
    before = (iota((32, 32), 1) < iota((32, 32), 0)).astype(BF)
    rank = jnp.dot(before, inside.astype(BF), preferred_element_type=F32)
    weight = jnp.where(first, columns[:, 2:3], 0.0) + jnp.where(second, columns[:, 3:4], 0.0)
    mix = jnp.where((rank == place) & (inside > 0.0), weight, 0.0)
    high = mix.astype(BF)
    mix_ref[0:32] = high
    mix_ref[32:64] = (mix - high.astype(F32)).astype(BF)


def up_kernel(slots_ref, gate_ref, up_ref, out_ref):
    slots = slots_ref[...].reshape(256, 768)
    for pair in range(SIDE // 2):
        cols = slice(256 * pair, 256 * pair + 256)
        for half, ref in enumerate((gate_ref, up_ref)):
            part = jnp.dot(slots, ref[0, :, cols], preferred_element_type=F32).astype(BF)
            out_ref[2 * pair, :, 128 * half : 128 * half + 128] = part[:, 0:128]
            out_ref[2 * pair + 1, :, 128 * half : 128 * half + 128] = part[:, 128:256]


def hidden_kernel(parts_ref, out_ref):
    total = parts_ref[0].astype(F32)
    for s in range(1, SIDE):
        total = total + parts_ref[s].astype(F32)
    gate, up = total[:, 0:128], total[:, 128:256]
    hidden = (gate / (1.0 + jnp.exp(-gate)) * up).astype(BF)
    for s in range(SIDE):
        out_ref[s] = hidden


def down_kernel(hidden_ref, down_ref, out_ref):
    hidden = jnp.concatenate([hidden_ref[s] for s in range(SIDE)], axis=1)
    out = jnp.dot(hidden, down_ref[0], preferred_element_type=F32)
    out_ref[...] = out.astype(BF).reshape(32, 8, 768)


def mix_kernel(mix_ref, parts_ref, out_ref):
    both = jnp.dot(mix_ref[...], parts_ref[...].reshape(256, 768), preferred_element_type=F32)
    both = both[0:32] + both[32:64]
    out_ref[0] = both[0:8]
    out_ref[1] = both[16:24]


def local(rows, expert_ids, combine, w_gate, w_up, w_down):
    width = rows.shape[1]
    core = lax.axis_index("core").astype(jnp.int32)
    ids, weights = expert_ids.T.astype(F32), combine.T
    meta = jnp.concatenate([ids, weights, jnp.zeros((4, TOK), F32)], axis=0)
    meta = jnp.concatenate([meta, jnp.zeros((8, 8), F32), meta, jnp.zeros((8, width - 24), F32)], axis=1)
    mine = jnp.concatenate([rows.astype(F32), meta], axis=0)
    both = lax.all_gather(mine, "core", axis=0, tiled=True)
    slots, mix = pl.pallas_call(
        route_kernel,
        out_shape=(
            jax.ShapeDtypeStruct((32, 8, width), BF),
            jax.ShapeDtypeStruct((64, 256), BF),
        ),
        in_specs=[SM, VM],
        out_specs=(VM, VM),
        compiler_params=LIMIT,
    )(core.reshape(1), both)
    slots = lax.all_to_all(slots, ("host", "tp"), 0, 0, tiled=True)
    parts = pl.pallas_call(
        up_kernel,
        out_shape=jax.ShapeDtypeStruct((SIDE, 256, 256), BF),
        in_specs=[VM, VM, VM],
        out_specs=VM,
        compiler_params=LIMIT,
    )(slots, w_gate, w_up)
    parts = lax.all_to_all(parts, "side", 0, 0, tiled=True)
    hidden = pl.pallas_call(
        hidden_kernel,
        out_shape=jax.ShapeDtypeStruct((SIDE, 256, 128), BF),
        in_specs=[VM],
        out_specs=VM,
        compiler_params=LIMIT,
    )(parts)
    hidden = lax.all_to_all(hidden, "side", 0, 0, tiled=True)
    outs = pl.pallas_call(
        down_kernel,
        out_shape=jax.ShapeDtypeStruct((32, 8, width), BF),
        in_specs=[VM, VM],
        out_specs=VM,
        compiler_params=LIMIT,
    )(hidden, w_down)
    outs = lax.all_to_all(outs, ("host", "tp"), 0, 0, tiled=True)
    mixed = pl.pallas_call(
        mix_kernel,
        out_shape=jax.ShapeDtypeStruct((2, TOK, width), F32),
        in_specs=[VM, VM],
        out_specs=VM,
        compiler_params=LIMIT,
    )(mix, outs)
    mixed = lax.all_gather(mixed, "core", axis=0)
    mixed = lax.dynamic_index_in_dim(mixed, core, 1, False)
    return (mixed[0] + mixed[1]).astype(BF)


def solution(mesh):
    fine = Mesh(mesh.devices.reshape(SIDE, HOSTS, CORES, TP), ("side", "host", "core", "tp"))
    tokens = ("host", "core", "tp")
    experts = ("host", "core")
    return jax.shard_map(
        local,
        mesh=fine,
        in_specs=(
            P(tokens, "side"),
            P(tokens, None),
            P(tokens, None),
            P(experts, "side", "tp"),
            P(experts, "side", "tp"),
            P(experts, "tp", "side"),
        ),
        out_specs=P(tokens, "side"),
        check_vma=False,
    )
```

```python
import functools

import jax
import jax.numpy as jnp
from jax import lax
from jax.experimental import pallas as pl
from jax.experimental.pallas import tpu as pltpu
from jax.sharding import Mesh
from jax.sharding import PartitionSpec as P

BF, F32 = jnp.bfloat16, jnp.float32
VM = pl.BlockSpec(memory_space=pltpu.VMEM)
SM = pl.BlockSpec(memory_space=pltpu.SMEM)
HBM = pl.BlockSpec(memory_space=pltpu.HBM)
LIMIT = pltpu.CompilerParams(vmem_limit_bytes=24 * 1024 * 1024)
CORES, HOSTS, TP, SIDE = 2, 4, 8, 8
TOK, CAP = 8, 4


def far(array):
    return pltpu.with_memory_space_constraint(array, pltpu.HBM)


def near(array):
    return pltpu.with_memory_space_constraint(array, pltpu.VMEM)


def iota(shape, dim):
    return lax.broadcasted_iota(jnp.int32, shape, dim)


def pack_kernel(rows_ref, ids_ref, weights_ref, out_ref):
    out_ref[0:8] = rows_ref[...].astype(F32)
    out_ref[8:16] = jnp.zeros((8, out_ref.shape[1]), F32)
    out_ref[8:10, 0:TOK] = ids_ref[...].astype(F32)
    out_ref[10:12, 0:TOK] = weights_ref[...]


def route_kernel(core_ref, both_ref, gate_hbm, up_hbm, out_ref, mix_ref):
    core = core_ref[0]
    both = both_ref[...]
    meta = jnp.where(iota((8, 128), 1) < 16, both[8:16, 0:128], pltpu.roll(both[24:32, 0:128], 16, 1))
    real = (iota((8, 128), 1) % 16 < TOK) & (iota((8, 128), 1) < 32)
    meta = jnp.where(real, meta, -1.0)
    row = iota((32, 128), 0)
    expert = (2 * (row // 8) + core).astype(F32)
    group, place = (row // CAP) % 2, (row % CAP).astype(F32)
    inside = ((meta[0:1] == expert) | (meta[1:2] == expert)) & (iota((32, 128), 1) // 16 == group)
    inside = inside.astype(F32)
    before = (iota((128, 128), 0) < iota((128, 128), 1)).astype(BF)
    rank = jnp.dot(inside.astype(BF), before, preferred_element_type=F32)
    pick = jnp.where(rank == place, inside, 0.0).astype(BF)
    slots = jnp.dot(pick[:, 0:32], both.astype(BF), preferred_element_type=F32)
    for h in range(HOSTS):
        mine = slots[8 * h : 8 * h + 8].astype(BF)
        for t in range(TP):
            out_ref[TP * h + t] = mine
    columns = jnp.transpose(meta)[0:32]
    spot = iota((32, 256), 1)
    expert = (2 * (spot // 64) + core).astype(F32)
    group, place = (spot // CAP) % 2, (spot % CAP).astype(F32)
    first, second = columns[:, 0:1] == expert, columns[:, 1:2] == expert
    inside = ((first | second) & (iota((32, 256), 0) // 16 == group)).astype(F32)
    before = (iota((32, 32), 1) < iota((32, 32), 0)).astype(BF)
    rank = jnp.dot(before, inside.astype(BF), preferred_element_type=F32)
    weight = jnp.where(first, columns[:, 2:3], 0.0) + jnp.where(second, columns[:, 3:4], 0.0)
    mix = jnp.where((rank == place) & (inside > 0.0), weight, 0.0)
    high = mix.astype(BF)
    mix_ref[0:32] = high
    mix_ref[32:64] = (mix - high.astype(F32)).astype(BF)


def up_kernel(slots_ref, gate_ref, up_ref, out_ref):
    slots = slots_ref[...].reshape(256, 768)
    for pair in range(SIDE // 2):
        cols = slice(256 * pair, 256 * pair + 256)
        for half, ref in enumerate((gate_ref, up_ref)):
            part = jnp.dot(slots, ref[0, :, cols], preferred_element_type=F32).astype(BF)
            out_ref[2 * pair, :, 128 * half : 128 * half + 128] = part[:, 0:128]
            out_ref[2 * pair + 1, :, 128 * half : 128 * half + 128] = part[:, 128:256]


def hidden_kernel(parts_ref, out_ref):
    total = parts_ref[0].astype(F32)
    for s in range(1, SIDE):
        total = total + parts_ref[s].astype(F32)
    gate, up = total[:, 0:128], total[:, 128:256]
    hidden = (gate / (1.0 + jnp.exp(-gate)) * up).astype(BF)
    for s in range(SIDE):
        out_ref[s] = hidden


def down_kernel(hidden_ref, down_ref, out_ref):
    hidden = jnp.concatenate([hidden_ref[s] for s in range(SIDE)], axis=1)
    out = jnp.dot(hidden, down_ref[0], preferred_element_type=F32)
    out_ref[...] = out.astype(BF).reshape(32, 8, 768)


def mix_kernel(mix_ref, parts_ref, out_ref):
    both = jnp.dot(mix_ref[...], parts_ref[...].reshape(256, 768), preferred_element_type=F32)
    both = both[0:32] + both[32:64]
    out_ref[0] = both[0:8]
    out_ref[1] = both[16:24]


def add_kernel(core_ref, both_ref, out_ref):
    core = core_ref[0]
    out_ref[...] = (both_ref[core] + both_ref[2 + core]).astype(BF)


def local(rows, expert_ids, combine, w_gate, w_up, w_down):
    width = rows.shape[1]
    core = lax.axis_index("core").astype(jnp.int32).reshape(1)
    mine = pl.pallas_call(
        pack_kernel,
        out_shape=jax.ShapeDtypeStruct((16, width), F32),
        in_specs=[VM, VM, VM],
        out_specs=VM,
        compiler_params=LIMIT,
    )(far(rows), far(expert_ids.T), far(combine.T))
    both = lax.all_gather(mine, "core", axis=0, tiled=True)
    slots, mix = pl.pallas_call(
        route_kernel,
        out_shape=(
            jax.ShapeDtypeStruct((32, 8, width), BF),
            jax.ShapeDtypeStruct((64, 256), BF),
        ),
        in_specs=[SM, VM, HBM, HBM],
        out_specs=(VM, VM),
        compiler_params=LIMIT,
    )(core, both, far(w_gate), far(w_up))
    slots = lax.all_to_all(slots, ("host", "tp"), 0, 0, tiled=True)
    parts = pl.pallas_call(
        up_kernel,
        out_shape=jax.ShapeDtypeStruct((SIDE, 256, 256), BF),
        in_specs=[VM, VM, VM],
        out_specs=VM,
        compiler_params=LIMIT,
    )(slots, near(w_gate), near(w_up))
    parts = lax.all_to_all(parts, "side", 0, 0, tiled=True)
    hidden = pl.pallas_call(
        hidden_kernel,
        out_shape=jax.ShapeDtypeStruct((SIDE, 256, 128), BF),
        in_specs=[VM],
        out_specs=VM,
        compiler_params=LIMIT,
    )(parts)
    hidden = lax.all_to_all(hidden, "side", 0, 0, tiled=True)
    outs = pl.pallas_call(
        down_kernel,
        out_shape=jax.ShapeDtypeStruct((32, 8, width), BF),
        in_specs=[VM, VM],
        out_specs=VM,
        compiler_params=LIMIT,
    )(hidden, w_down)
    outs = lax.all_to_all(outs, ("host", "tp"), 0, 0, tiled=True)
    mixed = pl.pallas_call(
        mix_kernel,
        out_shape=jax.ShapeDtypeStruct((2, TOK, width), F32),
        in_specs=[VM, VM],
        out_specs=VM,
        compiler_params=LIMIT,
    )(mix, outs)
    mixed = lax.all_gather(mixed, "core", axis=0, tiled=True)
    return pl.pallas_call(
        add_kernel,
        out_shape=jax.ShapeDtypeStruct((TOK, width), BF),
        in_specs=[SM, VM],
        out_specs=VM,
        compiler_params=LIMIT,
    )(core, mixed)


def solution(mesh):
    fine = Mesh(mesh.devices.reshape(SIDE, HOSTS, CORES, TP), ("side", "host", "core", "tp"))
    tokens = ("host", "core", "tp")
    experts = ("host", "core")
    return jax.shard_map(
        local,
        mesh=fine,
        in_specs=(
            P(tokens, "side"),
            P(tokens, None),
            P(tokens, None),
            P(experts, "side", "tp"),
            P(experts, "side", "tp"),
            P(experts, "tp", "side"),
        ),
        out_specs=P(tokens, "side"),
        check_vma=False,
    )
```

```python
import functools

import jax
import jax.numpy as jnp
from jax import lax
from jax.experimental import pallas as pl
from jax.experimental.pallas import tpu as pltpu
from jax.sharding import Mesh
from jax.sharding import PartitionSpec as P

BF, F32 = jnp.bfloat16, jnp.float32
VM = pl.BlockSpec(memory_space=pltpu.VMEM)
SM = pl.BlockSpec(memory_space=pltpu.SMEM)
HBM = pl.BlockSpec(memory_space=pltpu.HBM)
LIMIT = pltpu.CompilerParams(vmem_limit_bytes=24 * 1024 * 1024)
CORES, HOSTS, TP, SIDE = 2, 4, 8, 8
TOK, CAP = 8, 4
FEW = 128
EMPTY = 64.0


def far(array):
    return pltpu.with_memory_space_constraint(array, pltpu.HBM)


def near(array):
    return pltpu.with_memory_space_constraint(array, pltpu.VMEM)


def iota(shape, dim):
    return lax.broadcasted_iota(jnp.int32, shape, dim)


def pack_kernel(rows_ref, ids_ref, weights_ref, out_ref):
    out_ref[0:8] = rows_ref[...].astype(F32)
    out_ref[8:16] = jnp.zeros((8, out_ref.shape[1]), F32)
    out_ref[8:10, 0:TOK] = ids_ref[...].astype(F32)
    out_ref[10:12, 0:TOK] = weights_ref[...]


def route_kernel(core_ref, both_ref, gate_hbm, up_hbm, out_ref, mix_ref):
    core = core_ref[0]
    both = both_ref[...]
    meta = jnp.where(iota((8, 128), 1) < 16, both[8:16, 0:128], pltpu.roll(both[24:32, 0:128], 16, 1))
    real = (iota((8, 128), 1) % 16 < TOK) & (iota((8, 128), 1) < 32)
    meta = jnp.where(real, meta, -1.0)
    row = iota((32, 128), 0)
    expert = (2 * (row // 8) + core).astype(F32)
    group, place = (row // CAP) % 2, (row % CAP).astype(F32)
    inside = ((meta[0:1] == expert) | (meta[1:2] == expert)) & (iota((32, 128), 1) // 16 == group)
    inside = inside.astype(F32)
    before = (iota((128, 128), 0) < iota((128, 128), 1)).astype(BF)
    rank = jnp.dot(inside.astype(BF), before, preferred_element_type=F32)
    pick = jnp.where(rank == place, inside, 0.0)
    slots = jnp.dot(pick.astype(BF)[:, 0:32], both.astype(BF), preferred_element_type=F32)
    empty = 1.0 - jnp.sum(pick, axis=1, keepdims=True)
    slots = slots + jnp.where(iota(slots.shape, 1) == 0, EMPTY * empty, 0.0)
    for h in range(HOSTS):
        mine = slots[8 * h : 8 * h + 8].astype(BF)
        for t in range(TP):
            out_ref[TP * h + t] = mine
    columns = jnp.transpose(meta)[0:32]
    spot = iota((32, 256), 1)
    expert = (2 * (spot // 64) + core).astype(F32)
    group, place = (spot // CAP) % 2, (spot % CAP).astype(F32)
    first, second = columns[:, 0:1] == expert, columns[:, 1:2] == expert
    inside = ((first | second) & (iota((32, 256), 0) // 16 == group)).astype(F32)
    before = (iota((32, 32), 1) < iota((32, 32), 0)).astype(BF)
    rank = jnp.dot(before, inside.astype(BF), preferred_element_type=F32)
    weight = jnp.where(first, columns[:, 2:3], 0.0) + jnp.where(second, columns[:, 3:4], 0.0)
    mix = jnp.where((rank == place) & (inside > 0.0), weight, 0.0)
    high = mix.astype(BF)
    mix_ref[0:32] = high
    mix_ref[32:64] = (mix - high.astype(F32)).astype(BF)


def up_kernel(slots_ref, gate_ref, up_ref, down_hbm, out_ref, spread_ref, count_ref):
    slots = slots_ref[...].reshape(256, 768)
    used = (slots[:, 0:1].astype(F32) < EMPTY / 2).astype(F32)
    count_ref[0] = jnp.sum(used).astype(jnp.int32)
    wide = jnp.broadcast_to(used, (256, 256))
    row, col = iota((256, 256), 0), iota((256, 256), 1)
    ones = jnp.ones((8, 256), BF)
    rank = jnp.dot(ones, jnp.where(row < col, wide, 0.0).astype(BF), preferred_element_type=F32)[0:1]
    here = jnp.dot(ones, jnp.where(row == col, wide, 0.0).astype(BF), preferred_element_type=F32)[0:1]
    front = jnp.where(row.astype(F32) == rank, here, 0.0).astype(BF)
    slots = jnp.dot(front, slots, preferred_element_type=F32).astype(BF)
    before = jnp.where(col < row, 1.0, 0.0).astype(BF)
    rank = jnp.dot(before, wide.astype(BF), preferred_element_type=F32)
    spread_ref[...] = jnp.where(rank == col.astype(F32), wide, 0.0).astype(BF)
    for pair in range(SIDE // 2):
        cols = slice(256 * pair, 256 * pair + 256)
        for half, ref in enumerate((gate_ref, up_ref)):
            part = jnp.dot(slots, ref[0, :, cols], preferred_element_type=F32).astype(BF)
            out_ref[2 * pair, :, 128 * half : 128 * half + 128] = part[:, 0:128]
            out_ref[2 * pair + 1, :, 128 * half : 128 * half + 128] = part[:, 128:256]


def hidden_kernel(parts_ref, out_ref):
    total = parts_ref[0].astype(F32)
    for s in range(1, SIDE):
        total = total + parts_ref[s].astype(F32)
    gate, up = total[:, 0:128], total[:, 128:256]
    hidden = (gate / (1.0 + jnp.exp(-gate)) * up).astype(BF)
    for s in range(SIDE):
        out_ref[s] = hidden


def down_kernel(hidden_ref, spread_ref, down_ref, out_ref):
    hidden = jnp.concatenate([hidden_ref[s] for s in range(SIDE)], axis=1)
    out = jnp.dot(hidden, down_ref[0], preferred_element_type=F32).astype(BF)
    out = jnp.dot(spread_ref[...], out, preferred_element_type=F32)
    out_ref[...] = out.astype(BF).reshape(32, 8, 768)


def mix_kernel(mix_ref, parts_ref, out_ref):
    both = jnp.dot(mix_ref[...], parts_ref[...].reshape(256, 768), preferred_element_type=F32)
    both = both[0:32] + both[32:64]
    out_ref[0] = both[0:8]
    out_ref[1] = both[16:24]


def add_kernel(core_ref, both_ref, out_ref):
    core = core_ref[0]
    out_ref[...] = (both_ref[core] + both_ref[2 + core]).astype(BF)


def middle(parts):
    parts = lax.all_to_all(parts, "side", 0, 0, tiled=True)
    hidden = pl.pallas_call(
        hidden_kernel,
        out_shape=jax.ShapeDtypeStruct(parts.shape[:2] + (128,), BF),
        in_specs=[VM],
        out_specs=VM,
        compiler_params=LIMIT,
    )(parts)
    return lax.all_to_all(hidden, "side", 0, 0, tiled=True)


def few(parts):
    hidden = middle(parts[:, :FEW])
    return jnp.pad(hidden, ((0, 0), (0, 256 - FEW), (0, 0)))


def local(rows, expert_ids, combine, w_gate, w_up, w_down):
    width = rows.shape[1]
    core = lax.axis_index("core").astype(jnp.int32).reshape(1)
    mine = pl.pallas_call(
        pack_kernel,
        out_shape=jax.ShapeDtypeStruct((16, width), F32),
        in_specs=[VM, VM, VM],
        out_specs=VM,
        compiler_params=LIMIT,
    )(far(rows), far(expert_ids.T), far(combine.T))
    both = lax.all_gather(mine, "core", axis=0, tiled=True)
    slots, mix = pl.pallas_call(
        route_kernel,
        out_shape=(
            jax.ShapeDtypeStruct((32, 8, width), BF),
            jax.ShapeDtypeStruct((64, 256), BF),
        ),
        in_specs=[SM, VM, HBM, HBM],
        out_specs=(VM, VM),
        compiler_params=LIMIT,
    )(core, both, far(w_gate), far(w_up))
    slots = lax.all_to_all(slots, ("host", "tp"), 0, 0, tiled=True)
    parts, spread, count = pl.pallas_call(
        up_kernel,
        out_shape=(
            jax.ShapeDtypeStruct((SIDE, 256, 256), BF),
            jax.ShapeDtypeStruct((256, 256), BF),
            jax.ShapeDtypeStruct((1,), jnp.int32),
        ),
        in_specs=[VM, VM, VM, HBM],
        out_specs=(VM, VM, SM),
        compiler_params=LIMIT,
    )(slots, near(w_gate), near(w_up), far(w_down))
    hidden = lax.cond(count[0] <= FEW, few, middle, parts)
    outs = pl.pallas_call(
        down_kernel,
        out_shape=jax.ShapeDtypeStruct((32, 8, width), BF),
        in_specs=[VM, VM, VM],
        out_specs=VM,
        compiler_params=LIMIT,
    )(hidden, spread, near(w_down))
    outs = lax.all_to_all(outs, ("host", "tp"), 0, 0, tiled=True)
    mixed = pl.pallas_call(
        mix_kernel,
        out_shape=jax.ShapeDtypeStruct((2, TOK, width), F32),
        in_specs=[VM, VM],
        out_specs=VM,
        compiler_params=LIMIT,
    )(mix, outs)
    mixed = lax.all_gather(mixed, "core", axis=0, tiled=True)
    return pl.pallas_call(
        add_kernel,
        out_shape=jax.ShapeDtypeStruct((TOK, width), BF),
        in_specs=[SM, VM],
        out_specs=VM,
        compiler_params=LIMIT,
    )(core, mixed)


def solution(mesh):
    fine = Mesh(mesh.devices.reshape(SIDE, HOSTS, CORES, TP), ("side", "host", "core", "tp"))
    tokens = ("host", "core", "tp")
    experts = ("host", "core")
    return jax.shard_map(
        local,
        mesh=fine,
        in_specs=(
            P(tokens, "side"),
            P(tokens, None),
            P(tokens, None),
            P(experts, "side", "tp"),
            P(experts, "side", "tp"),
            P(experts, "tp", "side"),
        ),
        out_specs=P(tokens, "side"),
        check_vma=False,
    )
```

```python
import functools

import jax
import jax.numpy as jnp
from jax import lax
from jax.experimental import pallas as pl
from jax.experimental.pallas import tpu as pltpu
from jax.sharding import Mesh
from jax.sharding import PartitionSpec as P

BF, F32 = jnp.bfloat16, jnp.float32
VM = pl.BlockSpec(memory_space=pltpu.VMEM)
SM = pl.BlockSpec(memory_space=pltpu.SMEM)
HBM = pl.BlockSpec(memory_space=pltpu.HBM)
LIMIT = pltpu.CompilerParams(vmem_limit_bytes=24 * 1024 * 1024)
CORES, HOSTS, TP, SIDE = 2, 4, 8, 8
TOK, CAP = 8, 4
FEW = 128
EMPTY = 64.0


def far(array):
    return pltpu.with_memory_space_constraint(array, pltpu.HBM)


def near(array):
    return pltpu.with_memory_space_constraint(array, pltpu.VMEM)


def iota(shape, dim):
    return lax.broadcasted_iota(jnp.int32, shape, dim)


def pack_kernel(rows_ref, ids_ref, weights_ref, out_ref):
    out_ref[0:8] = rows_ref[...].astype(F32)
    out_ref[8:16] = jnp.zeros((8, out_ref.shape[1]), F32)
    out_ref[8:10, 0:TOK] = ids_ref[...].astype(F32)
    out_ref[10:12, 0:TOK] = weights_ref[...]


def route_kernel(core_ref, both_ref, gate_hbm, up_hbm, out_ref, mix_ref):
    core = core_ref[0]
    both = both_ref[...]
    meta = jnp.where(iota((8, 128), 1) < 16, both[8:16, 0:128], pltpu.roll(both[24:32, 0:128], 16, 1))
    real = (iota((8, 128), 1) % 16 < TOK) & (iota((8, 128), 1) < 32)
    meta = jnp.where(real, meta, -1.0)
    row = iota((32, 128), 0)
    expert = (2 * (row // 8) + core).astype(F32)
    group, place = (row // CAP) % 2, (row % CAP).astype(F32)
    inside = ((meta[0:1] == expert) | (meta[1:2] == expert)) & (iota((32, 128), 1) // 16 == group)
    inside = inside.astype(F32)
    before = (iota((128, 128), 0) < iota((128, 128), 1)).astype(BF)
    rank = jnp.dot(inside.astype(BF), before, preferred_element_type=F32)
    pick = jnp.where(rank == place, inside, 0.0)
    slots = jnp.dot(pick.astype(BF)[:, 0:32], both.astype(BF), preferred_element_type=F32)
    empty = 1.0 - jnp.sum(pick, axis=1, keepdims=True)
    slots = slots + jnp.where(iota(slots.shape, 1) == 0, EMPTY * empty, 0.0)
    for h in range(HOSTS):
        mine = slots[8 * h : 8 * h + 8].astype(BF)
        for t in range(TP):
            out_ref[TP * h + t] = mine
    columns = jnp.transpose(meta)[0:32]
    spot = iota((32, 256), 1)
    expert = (2 * (spot // 64) + core).astype(F32)
    group, place = (spot // CAP) % 2, (spot % CAP).astype(F32)
    first, second = columns[:, 0:1] == expert, columns[:, 1:2] == expert
    inside = ((first | second) & (iota((32, 256), 0) // 16 == group)).astype(F32)
    before = (iota((32, 32), 1) < iota((32, 32), 0)).astype(BF)
    rank = jnp.dot(before, inside.astype(BF), preferred_element_type=F32)
    weight = jnp.where(first, columns[:, 2:3], 0.0) + jnp.where(second, columns[:, 3:4], 0.0)
    mix = jnp.where((rank == place) & (inside > 0.0), weight, 0.0)
    high = mix.astype(BF)
    mix_ref[0:32] = high
    mix_ref[32:64] = (mix - high.astype(F32)).astype(BF)


def places(used):
    wide = jnp.broadcast_to(used, (256, 256))
    row, col = iota((256, 256), 0), iota((256, 256), 1)
    ones = jnp.ones((8, 256), BF)
    rank = jnp.dot(ones, jnp.where(row < col, wide, 0.0).astype(BF), preferred_element_type=F32)[0:1]
    here = jnp.dot(ones, jnp.where(row == col, wide, 0.0).astype(BF), preferred_element_type=F32)[0:1]
    front = jnp.where(row[0:FEW].astype(F32) == rank, here, 0.0).astype(BF)
    before = jnp.where(col < row, 1.0, 0.0).astype(BF)
    rank = jnp.dot(before, wide.astype(BF)[:, 0:FEW], preferred_element_type=F32)
    spread = jnp.where(rank == col[:, 0:FEW].astype(F32), wide[:, 0:FEW], 0.0).astype(BF)
    return front, spread


def up_kernel(slots_ref, gate_ref, up_ref, down_hbm, out_ref, few_ref, spread_ref, count_ref):
    slots = slots_ref[...].reshape(256, 768)
    used = (slots[:, 0:1].astype(F32) < EMPTY / 2).astype(F32)
    count = jnp.sum(used).astype(jnp.int32)
    count_ref[0] = count

    def parts(slots, ref_out):
        for pair in range(SIDE // 2):
            cols = slice(256 * pair, 256 * pair + 256)
            for half, ref in enumerate((gate_ref, up_ref)):
                part = jnp.dot(slots, ref[0, :, cols], preferred_element_type=F32).astype(BF)
                ref_out[2 * pair, :, 128 * half : 128 * half + 128] = part[:, 0:128]
                ref_out[2 * pair + 1, :, 128 * half : 128 * half + 128] = part[:, 128:256]

    @pl.when(count > FEW)
    def _():
        parts(slots, out_ref)

    @pl.when(count <= FEW)
    def _():
        front, spread = places(used)
        spread_ref[...] = spread
        parts(jnp.dot(front, slots, preferred_element_type=F32).astype(BF), few_ref)


def hidden_kernel(parts_ref, out_ref):
    total = parts_ref[0].astype(F32)
    for s in range(1, SIDE):
        total = total + parts_ref[s].astype(F32)
    gate, up = total[:, 0:128], total[:, 128:256]
    hidden = (gate / (1.0 + jnp.exp(-gate)) * up).astype(BF)
    for s in range(SIDE):
        out_ref[s] = hidden


def back_kernel(spread_ref, hidden_ref, out_ref):
    for s in range(SIDE):
        out_ref[s] = jnp.dot(spread_ref[...], hidden_ref[s], preferred_element_type=F32).astype(BF)


def down_kernel(hidden_ref, down_ref, out_ref):
    hidden = jnp.concatenate([hidden_ref[s] for s in range(SIDE)], axis=1)
    out = jnp.dot(hidden, down_ref[0], preferred_element_type=F32)
    out_ref[...] = out.astype(BF).reshape(32, 8, 768)


def mix_kernel(mix_ref, parts_ref, out_ref):
    both = jnp.dot(mix_ref[...], parts_ref[...].reshape(256, 768), preferred_element_type=F32)
    both = both[0:32] + both[32:64]
    out_ref[0] = both[0:8]
    out_ref[1] = both[16:24]


def add_kernel(core_ref, both_ref, out_ref):
    core = core_ref[0]
    out_ref[...] = (both_ref[core] + both_ref[2 + core]).astype(BF)


def middle(parts):
    parts = lax.all_to_all(parts, "side", 0, 0, tiled=True)
    hidden = pl.pallas_call(
        hidden_kernel,
        out_shape=jax.ShapeDtypeStruct(parts.shape[:2] + (128,), BF),
        in_specs=[VM],
        out_specs=VM,
        compiler_params=LIMIT,
    )(parts)
    return lax.all_to_all(hidden, "side", 0, 0, tiled=True)


def many(parts, few_parts, spread):
    return middle(parts)


def few(parts, few_parts, spread):
    return pl.pallas_call(
        back_kernel,
        out_shape=jax.ShapeDtypeStruct((SIDE, 256, 128), BF),
        in_specs=[VM, VM],
        out_specs=VM,
        compiler_params=LIMIT,
    )(spread, middle(few_parts))


def local(rows, expert_ids, combine, w_gate, w_up, w_down):
    width = rows.shape[1]
    core = lax.axis_index("core").astype(jnp.int32).reshape(1)
    mine = pl.pallas_call(
        pack_kernel,
        out_shape=jax.ShapeDtypeStruct((16, width), F32),
        in_specs=[VM, VM, VM],
        out_specs=VM,
        compiler_params=LIMIT,
    )(far(rows), far(expert_ids.T), far(combine.T))
    both = lax.all_gather(mine, "core", axis=0, tiled=True)
    slots, mix = pl.pallas_call(
        route_kernel,
        out_shape=(
            jax.ShapeDtypeStruct((32, 8, width), BF),
            jax.ShapeDtypeStruct((64, 256), BF),
        ),
        in_specs=[SM, VM, HBM, HBM],
        out_specs=(VM, VM),
        compiler_params=LIMIT,
    )(core, both, far(w_gate), far(w_up))
    slots = lax.all_to_all(slots, ("host", "tp"), 0, 0, tiled=True)
    parts, few_parts, spread, count = pl.pallas_call(
        up_kernel,
        out_shape=(
            jax.ShapeDtypeStruct((SIDE, 256, 256), BF),
            jax.ShapeDtypeStruct((SIDE, FEW, 256), BF),
            jax.ShapeDtypeStruct((256, FEW), BF),
            jax.ShapeDtypeStruct((1,), jnp.int32),
        ),
        in_specs=[VM, VM, VM, HBM],
        out_specs=(VM, VM, VM, SM),
        compiler_params=LIMIT,
    )(slots, near(w_gate), near(w_up), far(w_down))
    hidden = lax.cond(count[0] <= FEW, few, many, parts, few_parts, spread)
    outs = pl.pallas_call(
        down_kernel,
        out_shape=jax.ShapeDtypeStruct((32, 8, width), BF),
        in_specs=[VM, VM],
        out_specs=VM,
        compiler_params=LIMIT,
    )(hidden, near(w_down))
    outs = lax.all_to_all(outs, ("host", "tp"), 0, 0, tiled=True)
    mixed = pl.pallas_call(
        mix_kernel,
        out_shape=jax.ShapeDtypeStruct((2, TOK, width), F32),
        in_specs=[VM, VM],
        out_specs=VM,
        compiler_params=LIMIT,
    )(mix, outs)
    mixed = lax.all_gather(mixed, "core", axis=0, tiled=True)
    return pl.pallas_call(
        add_kernel,
        out_shape=jax.ShapeDtypeStruct((TOK, width), BF),
        in_specs=[SM, VM],
        out_specs=VM,
        compiler_params=LIMIT,
    )(core, mixed)


def solution(mesh):
    fine = Mesh(mesh.devices.reshape(SIDE, HOSTS, CORES, TP), ("side", "host", "core", "tp"))
    tokens = ("host", "core", "tp")
    experts = ("host", "core")
    return jax.shard_map(
        local,
        mesh=fine,
        in_specs=(
            P(tokens, "side"),
            P(tokens, None),
            P(tokens, None),
            P(experts, "side", "tp"),
            P(experts, "side", "tp"),
            P(experts, "tp", "side"),
        ),
        out_specs=P(tokens, "side"),
        check_vma=False,
    )
```

```python
import functools

import jax
import jax.numpy as jnp
from jax import lax
from jax.experimental import pallas as pl
from jax.experimental.pallas import tpu as pltpu
from jax.sharding import Mesh
from jax.sharding import PartitionSpec as P

BF, F32 = jnp.bfloat16, jnp.float32
VM = pl.BlockSpec(memory_space=pltpu.VMEM)
SM = pl.BlockSpec(memory_space=pltpu.SMEM)
HBM = pl.BlockSpec(memory_space=pltpu.HBM)
LIMIT = pltpu.CompilerParams(vmem_limit_bytes=24 * 1024 * 1024)
CORES, HOSTS, TP, SIDE = 2, 4, 8, 8
TOK, CAP = 8, 4
FEW = 128
EMPTY = 64.0


def far(array):
    return pltpu.with_memory_space_constraint(array, pltpu.HBM)


def near(array):
    return pltpu.with_memory_space_constraint(array, pltpu.VMEM)


def iota(shape, dim):
    return lax.broadcasted_iota(jnp.int32, shape, dim)


def pack_kernel(rows_ref, ids_ref, weights_ref, out_ref):
    out_ref[0:8] = rows_ref[...].astype(F32)
    out_ref[8:16] = jnp.zeros((8, out_ref.shape[1]), F32)
    out_ref[8:10, 0:TOK] = ids_ref[...].astype(F32)
    out_ref[10:12, 0:TOK] = weights_ref[...]


def route_kernel(core_ref, both_ref, gate_hbm, up_hbm, out_ref, mix_ref):
    core = core_ref[0]
    both = both_ref[...]
    meta = jnp.where(iota((8, 128), 1) < 16, both[8:16, 0:128], pltpu.roll(both[24:32, 0:128], 16, 1))
    real = (iota((8, 128), 1) % 16 < TOK) & (iota((8, 128), 1) < 32)
    meta = jnp.where(real, meta, -1.0)
    row = iota((32, 128), 0)
    expert = (2 * (row // 8) + core).astype(F32)
    group, place = (row // CAP) % 2, (row % CAP).astype(F32)
    inside = ((meta[0:1] == expert) | (meta[1:2] == expert)) & (iota((32, 128), 1) // 16 == group)
    inside = inside.astype(F32)
    before = (iota((128, 128), 0) < iota((128, 128), 1)).astype(BF)
    rank = jnp.dot(inside.astype(BF), before, preferred_element_type=F32)
    pick = jnp.where(rank == place, inside, 0.0)
    slots = jnp.dot(pick.astype(BF)[:, 0:32], both.astype(BF), preferred_element_type=F32)
    empty = 1.0 - jnp.sum(pick, axis=1, keepdims=True)
    slots = slots + jnp.where(iota(slots.shape, 1) == 0, EMPTY * empty, 0.0)
    for h in range(HOSTS):
        mine = slots[8 * h : 8 * h + 8].astype(BF)
        for t in range(TP):
            out_ref[TP * h + t] = mine
    columns = jnp.transpose(meta)[0:32]
    spot = iota((32, 256), 1)
    expert = (2 * (spot // 64) + core).astype(F32)
    group, place = (spot // CAP) % 2, (spot % CAP).astype(F32)
    first, second = columns[:, 0:1] == expert, columns[:, 1:2] == expert
    inside = ((first | second) & (iota((32, 256), 0) // 16 == group)).astype(F32)
    before = (iota((32, 32), 1) < iota((32, 32), 0)).astype(BF)
    rank = jnp.dot(before, inside.astype(BF), preferred_element_type=F32)
    weight = jnp.where(first, columns[:, 2:3], 0.0) + jnp.where(second, columns[:, 3:4], 0.0)
    mix = jnp.where((rank == place) & (inside > 0.0), weight, 0.0)
    high = mix.astype(BF)
    mix_ref[0:32] = high
    mix_ref[32:64] = (mix - high.astype(F32)).astype(BF)


def places(used):
    wide = jnp.broadcast_to(used, (256, 256))
    row, col = iota((256, 256), 0), iota((256, 256), 1)
    ones = jnp.ones((8, 256), BF)
    rank = jnp.dot(ones, jnp.where(row < col, wide, 0.0).astype(BF), preferred_element_type=F32)[0:1]
    here = jnp.dot(ones, jnp.where(row == col, wide, 0.0).astype(BF), preferred_element_type=F32)[0:1]
    front = jnp.where(row[0:FEW].astype(F32) == rank, here, 0.0).astype(BF)
    before = jnp.where(col < row, 1.0, 0.0).astype(BF)
    rank = jnp.dot(before, wide.astype(BF)[:, 0:FEW], preferred_element_type=F32)
    spread = jnp.where(rank == col[:, 0:FEW].astype(F32), wide[:, 0:FEW], 0.0).astype(BF)
    return front, spread


def up_kernel(slots_ref, gate_ref, up_ref, down_hbm, out_ref, few_ref, spread_ref, count_ref):
    slots = slots_ref[...].reshape(256, 768)
    used = (slots[:, 0:1].astype(F32) < EMPTY / 2).astype(F32)
    count = jnp.sum(used).astype(jnp.int32)
    count_ref[0] = count
    for pair in range(SIDE // 2):
        cols = slice(256 * pair, 256 * pair + 256)
        for half, ref in enumerate((gate_ref, up_ref)):
            part = jnp.dot(slots, ref[0, :, cols], preferred_element_type=F32).astype(BF)
            out_ref[2 * pair, :, 128 * half : 128 * half + 128] = part[:, 0:128]
            out_ref[2 * pair + 1, :, 128 * half : 128 * half + 128] = part[:, 128:256]

    @pl.when(count <= FEW)
    def _():
        front, spread = places(used)
        spread_ref[...] = spread
        for s in range(SIDE):
            few_ref[s] = jnp.dot(front, out_ref[s], preferred_element_type=F32).astype(BF)


def hidden_kernel(parts_ref, out_ref):
    total = parts_ref[0].astype(F32)
    for s in range(1, SIDE):
        total = total + parts_ref[s].astype(F32)
    gate, up = total[:, 0:128], total[:, 128:256]
    hidden = (gate / (1.0 + jnp.exp(-gate)) * up).astype(BF)
    for s in range(SIDE):
        out_ref[s] = hidden


def back_kernel(spread_ref, hidden_ref, out_ref):
    for s in range(SIDE):
        spread = spread_ref[:, 0 : hidden_ref.shape[1]]
        out_ref[s] = jnp.dot(spread, hidden_ref[s], preferred_element_type=F32).astype(BF)


def down_kernel(hidden_ref, down_ref, out_ref):
    hidden = jnp.concatenate([hidden_ref[s] for s in range(SIDE)], axis=1)
    out = jnp.dot(hidden, down_ref[0], preferred_element_type=F32)
    out_ref[...] = out.astype(BF).reshape(32, 8, 768)


def mix_kernel(mix_ref, parts_ref, out_ref):
    both = jnp.dot(mix_ref[...], parts_ref[...].reshape(256, 768), preferred_element_type=F32)
    both = both[0:32] + both[32:64]
    out_ref[0] = both[0:8]
    out_ref[1] = both[16:24]


def add_kernel(core_ref, both_ref, out_ref):
    core = core_ref[0]
    out_ref[...] = (both_ref[core] + both_ref[2 + core]).astype(BF)


def middle(parts):
    parts = lax.all_to_all(parts, "side", 0, 0, tiled=True)
    hidden = pl.pallas_call(
        hidden_kernel,
        out_shape=jax.ShapeDtypeStruct(parts.shape[:2] + (128,), BF),
        in_specs=[VM],
        out_specs=VM,
        compiler_params=LIMIT,
    )(parts)
    return lax.all_to_all(hidden, "side", 0, 0, tiled=True)


def many(parts, few_parts, spread):
    return middle(parts)


def few(rows, parts, few_parts, spread):
    return pl.pallas_call(
        back_kernel,
        out_shape=jax.ShapeDtypeStruct((SIDE, 256, 128), BF),
        in_specs=[VM, VM],
        out_specs=VM,
        compiler_params=LIMIT,
    )(spread, middle(few_parts[:, :rows]))


def local(rows, expert_ids, combine, w_gate, w_up, w_down):
    width = rows.shape[1]
    core = lax.axis_index("core").astype(jnp.int32).reshape(1)
    mine = pl.pallas_call(
        pack_kernel,
        out_shape=jax.ShapeDtypeStruct((16, width), F32),
        in_specs=[VM, VM, VM],
        out_specs=VM,
        compiler_params=LIMIT,
    )(far(rows), far(expert_ids.T), far(combine.T))
    both = lax.all_gather(mine, "core", axis=0, tiled=True)
    slots, mix = pl.pallas_call(
        route_kernel,
        out_shape=(
            jax.ShapeDtypeStruct((32, 8, width), BF),
            jax.ShapeDtypeStruct((64, 256), BF),
        ),
        in_specs=[SM, VM, HBM, HBM],
        out_specs=(VM, VM),
        compiler_params=LIMIT,
    )(core, both, far(w_gate), far(w_up))
    slots = lax.all_to_all(slots, ("host", "tp"), 0, 0, tiled=True)
    parts, few_parts, spread, count = pl.pallas_call(
        up_kernel,
        out_shape=(
            jax.ShapeDtypeStruct((SIDE, 256, 256), BF),
            jax.ShapeDtypeStruct((SIDE, FEW, 256), BF),
            jax.ShapeDtypeStruct((256, FEW), BF),
            jax.ShapeDtypeStruct((1,), jnp.int32),
        ),
        in_specs=[VM, VM, VM, HBM],
        out_specs=(VM, VM, VM, SM),
        compiler_params=LIMIT,
    )(slots, near(w_gate), near(w_up), far(w_down))
    size = (count[0] > FEW // 2).astype(jnp.int32) + (count[0] > FEW).astype(jnp.int32)
    sizes = [functools.partial(few, FEW // 2), functools.partial(few, FEW), many]
    hidden = lax.switch(size, sizes, parts, few_parts, spread)
    outs = pl.pallas_call(
        down_kernel,
        out_shape=jax.ShapeDtypeStruct((32, 8, width), BF),
        in_specs=[VM, VM],
        out_specs=VM,
        compiler_params=LIMIT,
    )(hidden, near(w_down))
    outs = lax.all_to_all(outs, ("host", "tp"), 0, 0, tiled=True)
    mixed = pl.pallas_call(
        mix_kernel,
        out_shape=jax.ShapeDtypeStruct((2, TOK, width), F32),
        in_specs=[VM, VM],
        out_specs=VM,
        compiler_params=LIMIT,
    )(mix, outs)
    mixed = lax.all_gather(mixed, "core", axis=0, tiled=True)
    return pl.pallas_call(
        add_kernel,
        out_shape=jax.ShapeDtypeStruct((TOK, width), BF),
        in_specs=[SM, VM],
        out_specs=VM,
        compiler_params=LIMIT,
    )(core, mixed)


def solution(mesh):
    fine = Mesh(mesh.devices.reshape(SIDE, HOSTS, CORES, TP), ("side", "host", "core", "tp"))
    tokens = ("host", "core", "tp")
    experts = ("host", "core")
    return jax.shard_map(
        local,
        mesh=fine,
        in_specs=(
            P(tokens, "side"),
            P(tokens, None),
            P(tokens, None),
            P(experts, "side", "tp"),
            P(experts, "side", "tp"),
            P(experts, "tp", "side"),
        ),
        out_specs=P(tokens, "side"),
        check_vma=False,
    )
```

```python
import functools

import jax
import jax.numpy as jnp
from jax import lax
from jax.experimental import pallas as pl
from jax.experimental.pallas import tpu as pltpu
from jax.sharding import Mesh
from jax.sharding import PartitionSpec as P

BF, F32 = jnp.bfloat16, jnp.float32
VM = pl.BlockSpec(memory_space=pltpu.VMEM)
SM = pl.BlockSpec(memory_space=pltpu.SMEM)
HBM = pl.BlockSpec(memory_space=pltpu.HBM)
LIMIT = pltpu.CompilerParams(vmem_limit_bytes=24 * 1024 * 1024)
CORES, HOSTS, TP, SIDE = 2, 4, 8, 8
TOK, CAP = 8, 4
FEW = 128
EMPTY = 64.0


def far(array):
    return pltpu.with_memory_space_constraint(array, pltpu.HBM)


def near(array):
    return pltpu.with_memory_space_constraint(array, pltpu.VMEM)


def iota(shape, dim):
    return lax.broadcasted_iota(jnp.int32, shape, dim)


def pack_kernel(rows_ref, ids_ref, weights_ref, out_ref):
    out_ref[0:8] = rows_ref[...].astype(F32)
    out_ref[8:16] = jnp.zeros((8, out_ref.shape[1]), F32)
    out_ref[8:10, 0:TOK] = ids_ref[...].astype(F32)
    out_ref[10:12, 0:TOK] = weights_ref[...]


def route_kernel(core_ref, both_ref, gate_hbm, up_hbm, out_ref, mix_ref):
    core = core_ref[0]
    both = both_ref[...]
    meta = jnp.where(iota((8, 128), 1) < 16, both[8:16, 0:128], pltpu.roll(both[24:32, 0:128], 16, 1))
    real = (iota((8, 128), 1) % 16 < TOK) & (iota((8, 128), 1) < 32)
    meta = jnp.where(real, meta, -1.0)
    row = iota((32, 128), 0)
    expert = (2 * (row // 8) + core).astype(F32)
    group, place = (row // CAP) % 2, (row % CAP).astype(F32)
    inside = ((meta[0:1] == expert) | (meta[1:2] == expert)) & (iota((32, 128), 1) // 16 == group)
    inside = inside.astype(F32)
    before = (iota((128, 128), 0) < iota((128, 128), 1)).astype(BF)
    rank = jnp.dot(inside.astype(BF), before, preferred_element_type=F32)
    pick = jnp.where(rank == place, inside, 0.0)
    slots = jnp.dot(pick.astype(BF)[:, 0:32], both.astype(BF), preferred_element_type=F32)
    empty = 1.0 - jnp.sum(pick, axis=1, keepdims=True)
    slots = slots + jnp.where(iota(slots.shape, 1) == 0, EMPTY * empty, 0.0)
    for h in range(HOSTS):
        mine = slots[8 * h : 8 * h + 8].astype(BF)
        for t in range(TP):
            out_ref[TP * h + t] = mine
    columns = jnp.transpose(meta)[0:32]
    spot = iota((32, 256), 1)
    expert = (2 * (spot // 64) + core).astype(F32)
    group, place = (spot // CAP) % 2, (spot % CAP).astype(F32)
    first, second = columns[:, 0:1] == expert, columns[:, 1:2] == expert
    inside = ((first | second) & (iota((32, 256), 0) // 16 == group)).astype(F32)
    before = (iota((32, 32), 1) < iota((32, 32), 0)).astype(BF)
    rank = jnp.dot(before, inside.astype(BF), preferred_element_type=F32)
    weight = jnp.where(first, columns[:, 2:3], 0.0) + jnp.where(second, columns[:, 3:4], 0.0)
    mix = jnp.where((rank == place) & (inside > 0.0), weight, 0.0)
    high = mix.astype(BF)
    mix_ref[0:32] = high
    mix_ref[32:64] = (mix - high.astype(F32)).astype(BF)


def places(used):
    wide = jnp.broadcast_to(used, (256, 256))
    row, col = iota((256, 256), 0), iota((256, 256), 1)
    ones = jnp.ones((8, 256), BF)
    rank = jnp.dot(ones, jnp.where(row < col, wide, 0.0).astype(BF), preferred_element_type=F32)[0:1]
    here = jnp.dot(ones, jnp.where(row == col, wide, 0.0).astype(BF), preferred_element_type=F32)[0:1]
    front = jnp.where(row[0:FEW].astype(F32) == rank, here, 0.0).astype(BF)
    before = jnp.where(col < row, 1.0, 0.0).astype(BF)
    rank = jnp.dot(before, wide.astype(BF)[:, 0:FEW], preferred_element_type=F32)
    spread = jnp.where(rank == col[:, 0:FEW].astype(F32), wide[:, 0:FEW], 0.0).astype(BF)
    return front, spread


def up_kernel(slots_ref, gate_ref, up_ref, down_hbm, out_ref, few_ref, spread_ref, count_ref):
    slots = slots_ref[...].reshape(256, 768)
    used = (slots[:, 0:1].astype(F32) < EMPTY / 2).astype(F32)
    count = jnp.sum(used).astype(jnp.int32)
    count_ref[0] = count
    for pair in range(SIDE // 2):
        cols = slice(256 * pair, 256 * pair + 256)
        for half, ref in enumerate((gate_ref, up_ref)):
            part = jnp.dot(slots, ref[0, :, cols], preferred_element_type=F32).astype(BF)
            out_ref[2 * pair, :, 128 * half : 128 * half + 128] = part[:, 0:128]
            out_ref[2 * pair + 1, :, 128 * half : 128 * half + 128] = part[:, 128:256]

    @pl.when(count <= FEW)
    def _():
        front, spread = places(used)
        spread_ref[...] = spread
        for s in range(SIDE):
            few_ref[s] = jnp.dot(front, out_ref[s], preferred_element_type=F32).astype(BF)


def hidden_kernel(parts_ref, out_ref):
    total = parts_ref[0].astype(F32)
    for s in range(1, SIDE):
        total = total + parts_ref[s].astype(F32)
    gate, up = total[:, 0:128], total[:, 128:256]
    hidden = (gate / (1.0 + jnp.exp(-gate)) * up).astype(BF)
    for s in range(SIDE):
        out_ref[s] = hidden


def back_kernel(spread_ref, hidden_ref, out_ref):
    for s in range(SIDE):
        out_ref[s] = jnp.dot(spread_ref[...], hidden_ref[s], preferred_element_type=F32).astype(BF)


def down_kernel(hidden_ref, down_ref, out_ref):
    hidden = jnp.concatenate([hidden_ref[s] for s in range(SIDE)], axis=1)
    out = jnp.dot(hidden, down_ref[0], preferred_element_type=F32)
    out_ref[...] = out.astype(BF).reshape(32, 8, 768)


def mix_kernel(mix_ref, parts_ref, out_ref):
    both = jnp.dot(mix_ref[...], parts_ref[...].reshape(256, 768), preferred_element_type=F32)
    both = both[0:32] + both[32:64]
    out_ref[0] = both[0:8]
    out_ref[1] = both[16:24]


def add_kernel(core_ref, both_ref, out_ref):
    core = core_ref[0]
    out_ref[...] = (both_ref[core] + both_ref[2 + core]).astype(BF)


def middle(parts):
    parts = lax.all_to_all(parts, "side", 0, 0, tiled=True)
    hidden = pl.pallas_call(
        hidden_kernel,
        out_shape=jax.ShapeDtypeStruct(parts.shape[:2] + (128,), BF),
        in_specs=[VM],
        out_specs=VM,
        compiler_params=LIMIT,
    )(parts)
    return lax.all_to_all(hidden, "side", 0, 0, tiled=True)


def many(parts, few_parts, spread):
    return middle(parts)


def few(parts, few_parts, spread):
    return pl.pallas_call(
        back_kernel,
        out_shape=jax.ShapeDtypeStruct((SIDE, 256, 128), BF),
        in_specs=[VM, VM],
        out_specs=VM,
        compiler_params=LIMIT,
    )(spread, middle(few_parts))


def local(rows, expert_ids, combine, w_gate, w_up, w_down):
    width = rows.shape[1]
    core = lax.axis_index("core").astype(jnp.int32).reshape(1)
    mine = pl.pallas_call(
        pack_kernel,
        out_shape=jax.ShapeDtypeStruct((16, width), F32),
        in_specs=[VM, VM, VM],
        out_specs=VM,
        compiler_params=LIMIT,
    )(far(rows), far(expert_ids.T), far(combine.T))
    both = lax.all_gather(mine, "core", axis=0, tiled=True)
    slots, mix = pl.pallas_call(
        route_kernel,
        out_shape=(
            jax.ShapeDtypeStruct((32, 8, width), BF),
            jax.ShapeDtypeStruct((64, 256), BF),
        ),
        in_specs=[SM, VM, HBM, HBM],
        out_specs=(VM, VM),
        compiler_params=LIMIT,
    )(core, both, far(w_gate), far(w_up))
    slots = lax.all_to_all(slots, ("host", "tp"), 0, 0, tiled=True)
    parts, few_parts, spread, count = pl.pallas_call(
        up_kernel,
        out_shape=(
            jax.ShapeDtypeStruct((SIDE, 256, 256), BF),
            jax.ShapeDtypeStruct((SIDE, FEW, 256), BF),
            jax.ShapeDtypeStruct((256, FEW), BF),
            jax.ShapeDtypeStruct((1,), jnp.int32),
        ),
        in_specs=[VM, VM, VM, HBM],
        out_specs=(VM, VM, VM, SM),
        compiler_params=LIMIT,
    )(slots, near(w_gate), near(w_up), far(w_down))
    hidden = lax.cond(count[0] <= FEW, few, many, parts, few_parts, spread)
    outs = pl.pallas_call(
        down_kernel,
        out_shape=jax.ShapeDtypeStruct((32, 8, width), BF),
        in_specs=[VM, VM],
        out_specs=VM,
        compiler_params=LIMIT,
    )(hidden, near(w_down))
    outs = lax.all_to_all(outs, ("host", "tp"), 0, 0, tiled=True)
    mixed = pl.pallas_call(
        mix_kernel,
        out_shape=jax.ShapeDtypeStruct((2, TOK, width), F32),
        in_specs=[VM, VM],
        out_specs=VM,
        compiler_params=LIMIT,
    )(mix, outs)
    mixed = lax.all_gather(mixed, "core", axis=0, tiled=True)
    return pl.pallas_call(
        add_kernel,
        out_shape=jax.ShapeDtypeStruct((TOK, width), BF),
        in_specs=[SM, VM],
        out_specs=VM,
        compiler_params=LIMIT,
    )(core, mixed)


def solution(mesh):
    fine = Mesh(mesh.devices.reshape(SIDE, HOSTS, CORES, TP), ("side", "host", "core", "tp"))
    tokens = ("host", "core", "tp")
    experts = ("host", "core")
    return jax.shard_map(
        local,
        mesh=fine,
        in_specs=(
            P(tokens, "side"),
            P(tokens, None),
            P(tokens, None),
            P(experts, "side", "tp"),
            P(experts, "side", "tp"),
            P(experts, "tp", "side"),
        ),
        out_specs=P(tokens, "side"),
        check_vma=False,
    )
```
